32 devices in a mesh: groups: 2 (over y), expert: 16 (over z, x, core).
Axes of the slice: x: 2, y: 2, z: 4, core: 2. Of those that a mesh axis runs over, the one named last changes fastest.
Arguments:
- output_gradient: bfloat16 [4096, 3584], P(('groups', 'expert')), parts along dimension 0, may hold values from -0.59765625 to 0.59765625
- activations: bfloat16 [4096, 3584], P(('groups', 'expert')), parts along dimension 0, may hold values from -1.5 to 1.5
- scores: float32 [4096, 8], P(('groups', 'expert')), parts along dimension 0, may hold values from 0.02 to 0.98
- chosen_expert_index: int32 [4096, 8], P(('groups', 'expert')), parts along dimension 0, may hold values from 0 to 15, all different within a row; in each aligned block of 128 rows (0 to 127, 128 to 255, ...) at most 80 rows name the same one
- frozen_down_weight: bfloat16 [16, 1024, 3584], P('expert'), may hold values from -0.1875 to 0.1875
- adapter_first: bfloat16 [16, 1024, 32], P('expert'), may hold values from -0.1875 to 0.1875
- adapter_second: bfloat16 [16, 32, 3584], P('expert'), may hold values from -1 to 1
- stored_hidden_rows: bfloat16 [32, 1280, 1024], P(('groups', 'expert')), parts along dimension 0, may hold values from -6 to 6
Outputs:
- chosen_score_gradient: float32 [4096, 8], P(('groups', 'expert')), parts along dimension 0
- adapter_first_gradient: float32 [32, 1024, 32], P(('groups', 'expert')), parts along dimension 0
- adapter_second_gradient: float32 [32, 32, 3584], P(('groups', 'expert')), parts along dimension 0
- router_weight_gradient: float32 [32, 3584], P(('groups', 'expert')), parts along dimension 0
The draws below stay inside these ranges and needn't reach their ends.
There are 2 independent parts, one for each index of `groups`. The reference program is written for one: setup_inputs(seed, part) draws one part's arguments, and reference() takes and returns one part's arrays. A program takes and returns all parts, laid end to end along the dimension named above; an argument that names none is the same for every part. Nothing has to cross between parts.
Inputs may be any that keep to these rules, and one draw needn't show every extreme that they name: `chosen_expert_index`: each row names 8 different experts. In the rows of one device no expert is named by more than 80 rows, a bound that some block reaches.
All inputs are finite; a program needn't handle non-finite values.
Results may differ from the reference program's by a relative error of at most 0.005.
Values may be sent and summed in bfloat16 or wider, within the bound.
A program may use at most 192 MiB of HBM per device.

```python
import math
import jax
import jax.numpy as jnp
import numpy as np
from jax import lax

MODEL_FEATURES = 3584
HIDDEN_UNITS = 1024
ADAPTER_RANK = 32
TOP = 8
TOK_DEV = 128
ROUTED_EXPERTS = 16
TOKENS = 2048
CAP = 80
N_EXPERT = 16


def levels(key, dims, cuts, low, top_value):
    def one(axis_at, blocks):
        heights = jax.random.uniform(jax.random.fold_in(jax.random.fold_in(key, 6), axis_at), (blocks,), jnp.float32, low / len(cuts), top_value / len(cuts))
        return jnp.repeat(jnp.exp(heights), dims[axis_at] // blocks).reshape((-1,) + (1,) * (len(dims) - axis_at - 1))

    loudness = one(*cuts[0])
    for cut in cuts[1:]:
        loudness = loudness * one(*cut)
    return loudness


def shared_out(own_key, own, number, rows, count, top, reach, skew):
    ranking = jax.random.permutation(own_key, count)
    packed, ordinary = shares(count, rows * top, reach, skew, True), shares(count, rows * top, reach, skew, False)
    places = jnp.arange(count)

    def named(tallies, turn):
        used = int((tallies > 0).sum())
        fixed = max(1, used // 4)
        moved = fixed + (places - fixed + turn * (used - fixed)) % max(1, count - fixed)
        return jnp.zeros((count,), jnp.int32).at[ranking[jnp.where(places < fixed, places, moved)]].set(jnp.asarray(tallies, jnp.int32))

    tallies = jnp.where(number % 4 == 0, named(packed, number // 4), named(ordinary, number - number // 4 - 1))
    mixed = jax.random.permutation(jax.random.fold_in(own, 3), count)
    source_of, taker = mixed[0:count // 2 * 2:2], mixed[1:count // 2 * 2:2]
    room = jnp.minimum(tallies[source_of] - 1, reach - tallies[taker]) // 2
    room = jnp.where((source_of == ranking[0]) | (taker == ranking[0]) | (tallies[taker] == 0), 0, jnp.maximum(room, 0))
    moved = jax.random.randint(jax.random.fold_in(own, 4), (count // 2,), 0, 1 << 20) % (room + 1)
    tallies = tallies.at[source_of].add(-moved).at[taker].add(moved)
    labels = jnp.searchsorted(jnp.cumsum(tallies), jnp.arange(rows * top), side="right").astype(jnp.int32)
    grid = labels.reshape(top, rows).T
    grid = grid[jax.random.permutation(jax.random.fold_in(own, 1), rows)]
    turn = jax.random.randint(jax.random.fold_in(own, 2), (rows, 1), 0, top)
    return jnp.take_along_axis(grid, (jnp.arange(top)[None, :] + turn) % top, axis=1)


def shares(amount, total, most, skew, full):
    weights = [(1 << 20) // math.isqrt(standing ** skew) + 1 for standing in range(1, amount + 1)]
    largest = most if full else min(most, max(-(-total // amount), total * weights[0] // sum(weights)))
    least = 1 if total - largest >= amount - 1 else 0
    holding, spare = [largest] + [least] * (amount - 1), total - largest - least * (amount - 1)
    while spare > 0:
        free = [i for i in range(1, amount) if holding[i] < largest] or [i for i in range(1, amount) if holding[i] < most]
        mass, remaining = sum([weights[i] for i in free]), spare
        for i in free:
            extra = min(most - holding[i], max(1, remaining * weights[i] // mass), spare)
            holding[i] = holding[i] + extra
            spare = spare - extra
    return np.array(holding)


def centred(stream_key, extent, deviation, most, cuts=(), kind=jnp.bfloat16):
    result = jax.random.normal(stream_key, extent, jnp.float32) * deviation
    if len(cuts) > 0:
        result = levels(stream_key, extent, cuts, -0.22, 0.18) * result
    return jnp.clip(result, min=-most, max=most).astype(kind)


def setup_inputs(seed: int = 0, part: int = 0) -> dict:
    seeds = jax.random.split(jax.random.key(seed), 9)
    part_splits = jax.random.split(jax.random.fold_in(seeds[8], part), 9)
    output_gradient = centred(part_splits[0], (TOKENS, MODEL_FEATURES), 0.1, 0.59765625, ((0, 16),))
    activations = centred(part_splits[1], (TOKENS, MODEL_FEATURES), 0.25, 1.5, ((0, 16),))
    scores = jnp.clip(jnp.exp(math.log(0.98) - 3.89182034 * jax.random.uniform(part_splits[2], (TOKENS, TOP), jnp.float32) ** levels(part_splits[2], (TOKENS, TOP), ((0, 16),), -0.2, 0.2)), 0.02, 0.98)
    chosen_expert_index_keys = jax.random.split(jax.random.fold_in(part_splits[3], 1), TOKENS // TOK_DEV)
    chosen_expert_index_turns = jax.random.permutation(jax.random.fold_in(part_splits[3], 3), TOKENS // TOK_DEV)
    chosen_expert_index = jax.vmap(lambda own, number: shared_out(jax.random.fold_in(part_splits[3], 2), own, number, TOK_DEV, ROUTED_EXPERTS, TOP, CAP, 2))(chosen_expert_index_keys, chosen_expert_index_turns).reshape((TOKENS, TOP))
    frozen_down_weight = centred(seeds[4], (ROUTED_EXPERTS, HIDDEN_UNITS, MODEL_FEATURES), HIDDEN_UNITS ** -0.5, 0.1875, ((0, 16),))
    adapter_first = centred(seeds[5], (ROUTED_EXPERTS, HIDDEN_UNITS, ADAPTER_RANK), HIDDEN_UNITS ** -0.5, 0.1875, ((0, 16),))
    adapter_second = centred(seeds[6], (ROUTED_EXPERTS, ADAPTER_RANK, MODEL_FEATURES), ADAPTER_RANK ** -0.5, 1.0, ((0, 16),))
    stored_hidden_rows = centred(part_splits[7], (ROUTED_EXPERTS, N_EXPERT * CAP, HIDDEN_UNITS), 1.0, 6.0, ((0, 16),))
    return {"output_gradient": output_gradient, "activations": activations, "scores": scores, "chosen_expert_index": chosen_expert_index, "frozen_down_weight": frozen_down_weight, "adapter_first": adapter_first, "adapter_second": adapter_second, "stored_hidden_rows": stored_hidden_rows}


adapter_scale = 2.0


def reference(output_gradient, activations, scores, chosen_expert_index, frozen_down_weight, adapter_first, adapter_second, stored_hidden_rows):
    score_sum = jnp.sum(scores, axis=1, keepdims=True)
    weights = scores / score_sum
    slot_weight = weights.astype(jnp.bfloat16)
    flat_ids = chosen_expert_index.reshape(N_EXPERT, TOK_DEV * TOP)
    one_hot = (flat_ids[:, :, None] == jnp.arange(ROUTED_EXPERTS, dtype=jnp.int32)[None, None, :]).astype(jnp.int32)
    slot_index = jnp.sum((jnp.cumsum(one_hot, axis=1) - 1) * one_hot, axis=2)
    slot_row = jnp.arange(N_EXPERT, dtype=jnp.int32)[:, None] * CAP + slot_index
    token_index = jnp.arange(TOKENS * TOP, dtype=jnp.int32) // TOP
    id_list = flat_ids.reshape(-1)
    row_list = slot_row.reshape(-1).astype(jnp.int32)
    lookup_matrix = jnp.full((ROUTED_EXPERTS, N_EXPERT * CAP), TOKENS, jnp.int32).at[id_list, row_list].set(token_index)
    scale_lookup_rows = jnp.zeros((ROUTED_EXPERTS, N_EXPERT * CAP), jnp.bfloat16).at[id_list, row_list].set(slot_weight.reshape(-1))
    padded_grad = jnp.concatenate([output_gradient, jnp.zeros((1, MODEL_FEATURES), jnp.bfloat16)], axis=0)

    def single_expert_step(items):
        picked, slot_scale, hidden_activation, expert_down_matrix, factor_a, second_factor = items
        slot_grad = padded_grad[picked]
        lowrank_hidden = jnp.dot(hidden_activation, factor_a, preferred_element_type=jnp.float32).astype(jnp.bfloat16)
        expert_output = jnp.dot(hidden_activation, expert_down_matrix, preferred_element_type=jnp.float32) + adapter_scale * jnp.dot(lowrank_hidden, second_factor, preferred_element_type=jnp.float32)
        slot_inner_product = jnp.sum(slot_grad.astype(jnp.float32) * expert_output, axis=1)
        scaled_output_gradient = (slot_scale.astype(jnp.float32)[:, None] * slot_grad.astype(jnp.float32)).astype(jnp.bfloat16)
        backward_lowrank = jnp.dot(scaled_output_gradient, second_factor.T, preferred_element_type=jnp.float32).astype(jnp.bfloat16)
        first_factor_gradient = adapter_scale * jnp.dot(hidden_activation.T, backward_lowrank, preferred_element_type=jnp.float32)
        second_factor_gradient = adapter_scale * jnp.dot(lowrank_hidden.T, scaled_output_gradient, preferred_element_type=jnp.float32)
        return slot_inner_product, first_factor_gradient, second_factor_gradient

    slot_inner_product, adapter_first_gradient, adapter_second_gradient = lax.map(single_expert_step, (lookup_matrix, scale_lookup_rows, stored_hidden_rows, frozen_down_weight, adapter_first, adapter_second))
    weight_grad = slot_inner_product[id_list, row_list].reshape(TOKENS, TOP)
    mixed = jnp.sum(weights * weight_grad, axis=1, keepdims=True)
    chosen_score_gradient = (weight_grad - mixed) / score_sum
    logit_grad = (chosen_score_gradient * scores * (1.0 - scores)).astype(jnp.bfloat16)
    token_rows = jnp.broadcast_to(jnp.arange(TOKENS, dtype=jnp.int32)[:, None], (TOKENS, TOP))
    router_matrix = jnp.zeros((ROUTED_EXPERTS, TOKENS), jnp.bfloat16).at[chosen_expert_index.reshape(-1), token_rows.reshape(-1)].set(logit_grad.reshape(-1))
    router_weight_gradient = jnp.dot(router_matrix, activations, preferred_element_type=jnp.float32)
    return (chosen_score_gradient, adapter_first_gradient, adapter_second_gradient, router_weight_gradient)
```

```python
import functools

import jax
import jax.numpy as jnp
from jax import lax
from jax.experimental import pallas as pl
from jax.experimental.pallas import tpu as pltpu
from jax.sharding import PartitionSpec as P

MESH = pl.DeviceIdType.MESH
adapter_scale = 2.0

NZ, NX, NC = 4, 2, 2
PARTS = 4
UP, DOWN, ACROSS, SIBLING = range(4)


def gather_kernel(
    grad_hbm, act_hbm, scores_ref, index_ref, weight_hbm, first_ref, second_ref, hidden_hbm,
    csg_ref, first_out, second_out, router_out,
    tokens, weight, hidden, act, expert_out, low, first_sum,
    table_send, table_recv, dot_send, dot_recv, router_send, router_recv,
    block_send_sem, block_recv_sem, table_send_sem, table_recv_sem,
    dot_send_sem, dot_recv_sem, router_send_sem, router_recv_sem, local_sem,
):
    n = NZ * NX * NC
    tok, feat = grad_hbm.shape
    top = scores_ref.shape[1]
    rank = second_ref.shape[0]
    units = weight.shape[0]
    cap = hidden.shape[0] // n
    rows = tok // PARTS
    me = lax.axis_index("expert")
    z, x, c = me // 4, (me // 2) % 2, me % 2
    f32, bf16 = jnp.float32, jnp.bfloat16

    barrier = pltpu.get_barrier_semaphore()

    def greet(i, _):
        pl.semaphore_signal(
            barrier, inc=1, device_id={"expert": (me + i) % n}, device_id_type=MESH
        )
        return 0

    local = [
        pltpu.make_async_copy(hidden_hbm, hidden, local_sem.at[0]),
        pltpu.make_async_copy(weight_hbm, weight, local_sem.at[1]),
        pltpu.make_async_copy(
            grad_hbm,
            tokens.at[z * 2 + x, pl.ds(pl.multiple_of(c * tok, tok), tok)],
            local_sem.at[2],
        ),
        pltpu.make_async_copy(act_hbm, act, local_sem.at[3]),
    ]
    for copy in local:
        copy.start()
    lax.fori_loop(1, n, greet, 0)
    pl.semaphore_wait(barrier, n - 1)

    def piece(zz, xx, cc, part):
        return tokens.at[
            zz * 2 + xx, pl.ds(pl.multiple_of(cc * tok + part * rows, rows), rows)
        ]

    def move(kind, zz, xx, cc, part, source=None):
        target = {
            UP: me + 4, DOWN: me - 4, ACROSS: z * 4 + (1 - x) * 2 + c, SIBLING: z * 4 + x * 2 + 1 - c,
        }[kind]
        block = zz * 4 + xx * 2 + cc
        place = piece(zz, xx, cc, part)
        return pltpu.make_async_remote_copy(
            src_ref=place if source is None else source,
            dst_ref=place,
            send_sem=block_send_sem.at[kind, block, part],
            recv_sem=block_recv_sem.at[block, part],
            device_id={"expert": target},
            device_id_type=MESH,
        )

    def own(part, act_on):
        source = grad_hbm.at[pl.ds(pl.multiple_of(part * rows, rows), rows)]
        act_on(move(ACROSS, z, x, c, part, source))

        @pl.when(z < NZ - 1)
        def _():
            act_on(move(UP, z, x, c, part, source))

        @pl.when(z > 0)
        def _():
            act_on(move(DOWN, z, x, c, part, source))

        act_on(move(SIBLING, z, x, c, part, source))

    def start(copy):
        copy.start()

    def sent(copy):
        copy.wait_send()

    def own_start(part, _):
        own(part, start)
        return 0

    lax.fori_loop(0, PARTS, own_start, 0)

    scores = jnp.transpose(scores_ref[...])
    index = jnp.transpose(index_ref[...])
    score_sum = jnp.sum(scores, axis=0, keepdims=True)
    weights = scores / score_sum
    expert_row = lax.broadcasted_iota(jnp.int32, (n, tok), 0)
    chosen = jnp.zeros((n, tok), f32)
    scale = jnp.zeros((n, tok), f32)
    for k in range(top):
        hit = index[k : k + 1, :] == expert_row
        chosen = jnp.where(hit, 1.0, chosen)
        scale = jnp.where(hit, weights[k : k + 1, :], scale)
    earlier = (
        lax.broadcasted_iota(jnp.int32, (tok, tok), 0)
        < lax.broadcasted_iota(jnp.int32, (tok, tok), 1)
    ).astype(bf16)
    slot = jnp.dot(chosen.astype(bf16), earlier, preferred_element_type=f32)
    slot = jnp.where(chosen > 0.5, slot, -1.0)
    scale = scale.astype(bf16).astype(f32)
    pad = jnp.zeros((6, tok), f32)
    for e in range(n):
        table_send[e] = jnp.concatenate([slot[e : e + 1], scale[e : e + 1], pad], axis=0)
    table_recv[me] = table_send[me]

    def table_copy(to, source):
        return pltpu.make_async_remote_copy(
            src_ref=table_send.at[to],
            dst_ref=table_recv.at[source],
            send_sem=table_send_sem.at[to],
            recv_sem=table_recv_sem.at[source],
            device_id={"expert": to},
            device_id_type=MESH,
        )

    def others(act_on):
        def body(i, _):
            act_on((me + i) % n)
            return 0

        lax.fori_loop(1, n, body, 0)

    others(lambda to: table_copy(to, me).start())

    local[0].wait()
    low[...] = jnp.dot(hidden[...], first_ref[...], preferred_element_type=f32).astype(bf16)
    local[1].wait()
    first_sum[...] = jnp.zeros_like(first_sum)
    second_out[...] = jnp.zeros_like(second_out)

    tile = 512
    tiles = feat // tile

    def output_tile(i):
        at = pl.ds(pl.multiple_of(i * tile, tile), tile)
        expert_out[:, at] = (
            jnp.dot(hidden[...], weight[:, at], preferred_element_type=f32)
            + adapter_scale
            * jnp.dot(low[...], second_ref[:, at], preferred_element_type=f32)
        ).astype(bf16)

    def dot_copy(to, source):
        return pltpu.make_async_remote_copy(
            src_ref=dot_send.at[to],
            dst_ref=dot_recv.at[source],
            send_sem=dot_send_sem.at[to],
            recv_sem=dot_recv_sem.at[source],
            device_id={"expert": to},
            device_id_type=MESH,
        )

    def chip(zz, xx):
        pair = zz * 2 + xx

        def arrived(part, _):
            move(SIBLING, zz, xx, 1 - c, part).wait_recv()
            return 0

        lax.fori_loop(0, PARTS, arrived, 0)
        both = tokens[pair]
        at = pl.ds(pl.multiple_of(pair * 2 * cap, 2 * cap), 2 * cap)
        nt = (((1,), (1,)), ((), ()))
        inner = lax.dot_general(expert_out[at, :], both, nt, preferred_element_type=f32)
        back = lax.dot_general(second_ref[...], both, nt, preferred_element_type=f32)
        t0, t1 = table_recv[2 * pair], table_recv[2 * pair + 1]
        slots = jnp.concatenate([t0[0:1], jnp.where(t1[0:1] < 0.0, -1.0, t1[0:1] + cap)], axis=1)
        scales = jnp.concatenate([t0[1:2], t1[1:2]], axis=1)
        number = lax.broadcasted_iota(jnp.int32, (2 * cap, 2 * tok), 0).astype(f32)
        match = number == slots
        dots = jnp.sum(jnp.where(match, inner, 0.0), axis=0, keepdims=True)
        for sub in range(2):
            to = 2 * pair + sub
            dot_send[to] = jnp.broadcast_to(dots[:, sub * tok : (sub + 1) * tok], (8, tok))

            @pl.when(to != me)
            def _():
                dot_copy(to, me).start()

            @pl.when(to == me)
            def _():
                dot_recv[to] = dot_send[to]

        one_hot = match.astype(bf16)
        back = (back * scales).astype(bf16)
        back = lax.dot_general(back, one_hot, nt, preferred_element_type=f32).astype(bf16)
        first_sum[...] += jnp.dot(back, hidden[at, :], preferred_element_type=f32)
        spread = lax.dot_general(
            low[at, :], one_hot, (((0,), (0,)), ((), ())), preferred_element_type=f32
        )
        spread = (adapter_scale * spread * scales).astype(bf16)
        second_out[...] += jnp.dot(spread, both, preferred_element_type=f32)

    def along(distance, part, act_on):
        @pl.when(z >= distance)
        def _():
            zz = z - distance
            act_on(zz, part, UP, z < NZ - 1)

        @pl.when(z + distance < NZ)
        def _():
            zz = z + distance
            act_on(zz, part, DOWN, z > 0)

    def pass_on(zz, part, kind, more):
        move(kind, zz, x, c, part).wait_recv()

        @pl.when(more)
        def _():
            move(kind, zz, x, c, part).start()

        move(ACROSS, zz, x, c, part).start()
        move(SIBLING, zz, x, c, part).start()

    def passed(zz, part, kind, more):
        @pl.when(more)
        def _():
            move(kind, zz, x, c, part).wait_send()

        move(ACROSS, zz, x, c, part).wait_send()
        move(SIBLING, zz, x, c, part).wait_send()

    def cross(zz, part, kind, more):
        move(ACROSS, zz, 1 - x, c, part).wait_recv()
        move(SIBLING, zz, 1 - x, c, part).start()

    def crossed(zz, part, kind, more):
        move(SIBLING, zz, 1 - x, c, part).wait_send()

    def chips_of(phase, which):
        side = which % 2
        distance = jnp.where(which < 2, phase, phase + 1)
        zz = jnp.where(side == 0, z - distance, z + distance)
        xx = jnp.where(which < 2, 1 - x, x)
        mine = (phase == 0) & (which == 1)
        xx = jnp.where(mine, x, xx)
        return zz, xx, (zz >= 0) & (zz < NZ)

    def first_phase(part, _):
        along(1, part, pass_on)
        for j in range(2):
            i = part * 2 + j

            @pl.when(i < tiles)
            def _():
                output_tile(i)

        cross(z, part, None, None)
        return 0

    lax.fori_loop(0, PARTS, first_phase, 0)
    local[2].wait()
    others(lambda source: table_copy(source, source).wait_recv())

    def later(step, _):
        phase, part = step // PARTS, step % PARTS

        along(phase + 1, part, pass_on)
        zz, xx, there = chips_of(phase - 1, part)

        @pl.when(there)
        def _():
            chip(zz, xx)

        along(phase, part, cross)
        return 0

    lax.fori_loop(PARTS, NZ * PARTS, later, 0)
    for side in range(2):
        zz, xx, there = chips_of(NZ - 1, side)

        @pl.when(there)
        def _():
            chip(zz, xx)

    first_out[...] = jnp.transpose(adapter_scale * first_sum[...])
    local[3].wait()
    others(lambda source: dot_copy(source, source).wait_recv())
    dots = dot_recv[:, 0, :]
    grads = []
    for k in range(top):
        hit = index[k : k + 1, :] == expert_row
        grads.append(jnp.sum(jnp.where(hit, dots, 0.0), axis=0, keepdims=True))
    weight_grad = jnp.concatenate(grads, axis=0)
    mixed = jnp.sum(weights * weight_grad, axis=0, keepdims=True)
    csg = (weight_grad - mixed) / score_sum
    csg_ref[...] = jnp.transpose(csg)
    logit = (csg * scores * (1.0 - scores)).astype(bf16).astype(f32)
    router = jnp.zeros((n, tok), f32)
    for k in range(top):
        router = jnp.where(index[k : k + 1, :] == expert_row, logit[k : k + 1, :], router)
    partial = jnp.dot(router.astype(bf16), act[...], preferred_element_type=f32)
    for j in range(feat // 128):
        router_send[:, j, :] = partial[:, j * 128 : (j + 1) * 128]
    router_recv[me] = router_send[me]

    def router_copy(to, source):
        return pltpu.make_async_remote_copy(
            src_ref=router_send.at[to],
            dst_ref=router_recv.at[source],
            send_sem=router_send_sem.at[to],
            recv_sem=router_recv_sem.at[source],
            device_id={"expert": to},
            device_id_type=MESH,
        )

    others(lambda to: router_copy(to, me).start())

    def drain(part, _):
        own(part, sent)
        crossed(z, part, None, None)
        return 0

    lax.fori_loop(0, PARTS, drain, 0)

    def drain_later(step, _):
        distance, part = step // PARTS, step % PARTS
        along(distance, part, passed)
        along(distance, part, crossed)
        return 0

    lax.fori_loop(PARTS, NZ * PARTS, drain_later, 0)
    others(lambda to: table_copy(to, me).wait_send())
    others(lambda to: dot_copy(to, me).wait_send())
    others(lambda source: router_copy(source, source).wait_recv())
    router_out[...] = jnp.sum(router_recv[...], axis=0)
    others(lambda to: router_copy(to, me).wait_send())


def per_device_gather(
    output_gradient, activations, scores, chosen_expert_index,
    frozen_down_weight, adapter_first, adapter_second, stored_hidden_rows,
):
    n = NZ * NX * NC
    tok, feat = output_gradient.shape
    units, rank = adapter_first.shape[1:]
    slots = stored_hidden_rows.shape[1]
    vmem = pl.BlockSpec(memory_space=pltpu.VMEM)
    hbm = pl.BlockSpec(memory_space=pl.ANY)
    f32, bf16 = jnp.float32, jnp.bfloat16
    dma = pltpu.SemaphoreType.DMA
    csg, first, second, router = pl.pallas_call(
        gather_kernel,
        out_shape=(
            jax.ShapeDtypeStruct(scores.shape, f32),
            jax.ShapeDtypeStruct((units, rank), f32),
            jax.ShapeDtypeStruct((rank, feat), f32),
            jax.ShapeDtypeStruct((feat // 128, 128), f32),
        ),
        in_specs=[hbm, hbm, vmem, vmem, hbm, vmem, vmem, hbm],
        out_specs=(vmem,) * 4,
        scratch_shapes=[
            pltpu.VMEM((NZ * NX, NC * tok, feat), bf16),
            pltpu.VMEM((units, feat), bf16),
            pltpu.VMEM((slots, units), bf16),
            pltpu.VMEM((tok, feat), bf16),
            pltpu.VMEM((slots, feat), bf16),
            pltpu.VMEM((slots, rank), bf16),
            pltpu.VMEM((rank, units), f32),
            pltpu.VMEM((n, 8, tok), f32),
            pltpu.VMEM((n, 8, tok), f32),
            pltpu.VMEM((n, 8, tok), f32),
            pltpu.VMEM((n, 8, tok), f32),
            pltpu.VMEM((n, feat // 128, 128), f32),
            pltpu.VMEM((n, feat // 128, 128), f32),
            dma((4, n, PARTS)),
            dma((n, PARTS)),
            dma((n,)),
            dma((n,)),
            dma((n,)),
            dma((n,)),
            dma((n,)),
            dma((n,)),
            dma((4,)),
        ],
        compiler_params=pltpu.CompilerParams(
            collective_id=0, has_side_effects=True, vmem_limit_bytes=60 * 1024 * 1024
        ),
        cost_estimate=pl.CostEstimate(
            flops=2 * slots * units * feat, bytes_accessed=2 * units * feat, transcendentals=0
        ),
    )(
        output_gradient, activations, scores, chosen_expert_index,
        frozen_down_weight[0], adapter_first[0], adapter_second[0], stored_hidden_rows[0],
    )
    return csg, first[None], second[None], router.reshape(1, feat)


def recompute_every_expert(hidden_activation, lowrank_hidden, expert_down_matrix, second_factor):
    return jnp.dot(
        hidden_activation, expert_down_matrix, preferred_element_type=jnp.float32
    ) + adapter_scale * jnp.dot(lowrank_hidden, second_factor, preferred_element_type=jnp.float32)


def per_device(
    output_gradient,
    activations,
    scores,
    chosen_expert_index,
    frozen_down_weight,
    adapter_first,
    adapter_second,
    stored_hidden_rows,
):
    devices = lax.axis_size("expert")
    exp_dev = frozen_down_weight.shape[0]
    slot_rows = stored_hidden_rows.shape[1]
    capacity = slot_rows // devices
    experts = exp_dev * devices
    tokens_dev = output_gradient.shape[0]
    chosen = scores.shape[1]
    features = output_gradient.shape[1]
    score_sum = jnp.sum(scores, axis=1, keepdims=True)
    weights = scores / score_sum
    slot_weight = weights.astype(jnp.bfloat16)
    flat_ids = chosen_expert_index.reshape(-1)
    one_hot = (flat_ids[:, None] == jnp.arange(experts, dtype=jnp.int32)[None, :]).astype(jnp.int32)
    slot_index = jnp.sum((jnp.cumsum(one_hot, axis=0) - 1) * one_hot, axis=1)
    position = flat_ids * capacity + slot_index
    repeated = jnp.repeat(output_gradient, chosen, axis=0)
    send_rows = jnp.zeros((experts * capacity, features), jnp.bfloat16).at[position].set(repeated)
    send_scale = (
        jnp.zeros((experts * capacity,), jnp.bfloat16).at[position].set(slot_weight.reshape(-1))
    )
    send_rows = send_rows.reshape(devices, exp_dev, capacity, features)
    send_scale = send_scale.reshape(devices, exp_dev, capacity)
    expert_number = 0
    hidden_activation = stored_hidden_rows[expert_number]
    lowrank_hidden = jnp.dot(
        hidden_activation, adapter_first[expert_number], preferred_element_type=jnp.float32
    ).astype(jnp.bfloat16)
    expert_output = recompute_every_expert(
        hidden_activation,
        lowrank_hidden,
        frozen_down_weight[expert_number],
        adapter_second[expert_number],
    )
    lows = [lowrank_hidden]
    outputs = [expert_output]
    recv_rows, recv_scale = (
        lax.all_to_all(send_rows, "expert", split_axis=0, concat_axis=0, tiled=True),
        lax.all_to_all(send_scale, "expert", split_axis=0, concat_axis=0, tiled=True),
    )
    expert_number = 0
    slot_grad = recv_rows[:, expert_number].reshape(slot_rows, features)
    slot_scale = recv_scale[:, expert_number].reshape(slot_rows)
    slot_inner_product = jnp.sum(slot_grad.astype(jnp.float32) * outputs[expert_number], axis=1)
    scaled_output_gradient = (
        slot_scale.astype(jnp.float32)[:, None] * slot_grad.astype(jnp.float32)
    ).astype(jnp.bfloat16)
    backward_lowrank = lax.dot_general(
        scaled_output_gradient,
        adapter_second[expert_number],
        (((1,), (1,)), ((), ())),
        preferred_element_type=jnp.float32,
    ).astype(jnp.bfloat16)
    first_factor_gradient = adapter_scale * lax.dot_general(
        stored_hidden_rows[expert_number],
        backward_lowrank,
        (((0,), (0,)), ((), ())),
        preferred_element_type=jnp.float32,
    )
    second_factor_gradient = adapter_scale * lax.dot_general(
        lows[expert_number],
        scaled_output_gradient,
        (((0,), (0,)), ((), ())),
        preferred_element_type=jnp.float32,
    )
    dots = [slot_inner_product.reshape(devices, capacity)]
    grads_a = [first_factor_gradient]
    grads_b = [second_factor_gradient]
    dot_table = jnp.stack(dots, axis=1)
    returned = lax.all_to_all(dot_table, "expert", split_axis=0, concat_axis=0, tiled=True)
    weight_grad = returned.reshape(experts * capacity)[position].reshape(tokens_dev, chosen)
    mixed = jnp.sum(weights * weight_grad, axis=1, keepdims=True)
    chosen_score_gradient = (weight_grad - mixed) / score_sum
    logit_grad = (chosen_score_gradient * scores * (1.0 - scores)).astype(jnp.bfloat16)
    matches = chosen_expert_index[None, :, :] == jnp.arange(experts, dtype=jnp.int32)[:, None, None]
    router_matrix = jnp.sum(
        jnp.where(matches, logit_grad.astype(jnp.float32)[None, :, :], 0.0), axis=2
    ).astype(jnp.bfloat16)
    router_weight_gradient = lax.psum_scatter(
        jnp.dot(router_matrix, activations, preferred_element_type=jnp.float32),
        "expert",
        scatter_dimension=0,
        tiled=True,
    )
    return (
        chosen_score_gradient,
        jnp.stack(grads_a, axis=0),
        jnp.stack(grads_b, axis=0),
        router_weight_gradient,
    )


def solution(mesh):
    placed = (
        P(("groups", "expert"), None),
        P(("groups", "expert"), None),
        P(("groups", "expert"), None),
        P(("groups", "expert"), None),
        P("expert", None, None),
        P("expert", None, None),
        P("expert", None, None),
        P(("groups", "expert"), None, None),
    )
    small = mesh.shape["expert"] == NZ * NX * NC
    return jax.shard_map(
        per_device_gather if small else per_device,
        mesh=mesh,
        in_specs=placed,
        out_specs=(
            P(("groups", "expert"), None),
            P(("groups", "expert"), None, None),
            P(("groups", "expert"), None, None),
            P(("groups", "expert"), None),
        ),
        check_vma=False,
    )
```

```python
import functools

import jax
import jax.numpy as jnp
from jax import lax
from jax.experimental import pallas as pl
from jax.experimental.pallas import tpu as pltpu
from jax.sharding import PartitionSpec as P

MESH = pl.DeviceIdType.MESH
adapter_scale = 2.0

NZ, NX, NC = 4, 2, 2
PARTS = 8
UP, DOWN, ACROSS, SIBLING = range(4)


def gather_kernel(
    grad_hbm, act_hbm, scores_ref, index_ref, weight_hbm, first_ref, second_ref, hidden_hbm,
    csg_ref, first_out, second_out, router_out,
    tokens, weight, hidden, act, expert_out, low, first_sum,
    table_send, table_recv, dot_send, dot_recv, router_sum, router_send, router_recv,
    block_send_sem, block_recv_sem, table_send_sem, table_recv_sem,
    dot_send_sem, dot_recv_sem, router_send_sem, router_recv_sem, local_sem,
):
    n = NZ * NX * NC
    tok, feat = grad_hbm.shape
    top = scores_ref.shape[0]
    rank = second_ref.shape[0]
    units = weight.shape[0]
    cap = hidden.shape[0] // n
    rows = tok // PARTS
    me = lax.axis_index("expert")
    z, x, c = me // 4, (me // 2) % 2, me % 2
    f32, bf16 = jnp.float32, jnp.bfloat16

    barrier = pltpu.get_barrier_semaphore()

    def greet(i, _):
        pl.semaphore_signal(
            barrier, inc=1, device_id={"expert": (me + i) % n}, device_id_type=MESH
        )
        return 0

    local = [
        pltpu.make_async_copy(hidden_hbm, hidden, local_sem.at[0]),
        pltpu.make_async_copy(weight_hbm, weight, local_sem.at[1]),
        pltpu.make_async_copy(
            grad_hbm,
            tokens.at[z * 2 + x, pl.ds(pl.multiple_of(c * tok, tok), tok)],
            local_sem.at[2],
        ),
        pltpu.make_async_copy(act_hbm, act, local_sem.at[3]),
    ]
    for copy in local:
        copy.start()
    lax.fori_loop(1, n, greet, 0)
    pl.semaphore_wait(barrier, n - 1)

    def piece(zz, xx, cc, part):
        return tokens.at[
            zz * 2 + xx, pl.ds(pl.multiple_of(cc * tok + part * rows, rows), rows)
        ]

    def move(kind, zz, xx, cc, part, source=None):
        target = {
            UP: me + 4, DOWN: me - 4, ACROSS: z * 4 + (1 - x) * 2 + c, SIBLING: z * 4 + x * 2 + 1 - c,
        }[kind]
        block = zz * 4 + xx * 2 + cc
        place = piece(zz, xx, cc, part)
        return pltpu.make_async_remote_copy(
            src_ref=place if source is None else source,
            dst_ref=place,
            send_sem=block_send_sem.at[kind, block, part],
            recv_sem=block_recv_sem.at[block, part],
            device_id={"expert": target},
            device_id_type=MESH,
        )

    def own(part, act_on):
        source = grad_hbm.at[pl.ds(pl.multiple_of(part * rows, rows), rows)]
        act_on(move(ACROSS, z, x, c, part, source))

        @pl.when(z < NZ - 1)
        def _():
            act_on(move(UP, z, x, c, part, source))

        @pl.when(z > 0)
        def _():
            act_on(move(DOWN, z, x, c, part, source))

        act_on(move(SIBLING, z, x, c, part, source))

    def start(copy):
        copy.start()

    def sent(copy):
        copy.wait_send()

    def own_start(part, _):
        own(part, start)
        return 0

    lax.fori_loop(0, PARTS, own_start, 0)

    scores = scores_ref[...]
    index = index_ref[...]
    score_sum = jnp.sum(scores, axis=0, keepdims=True)
    weights = scores / score_sum
    expert_row = lax.broadcasted_iota(jnp.int32, (n, tok), 0)
    chosen = jnp.zeros((n, tok), f32)
    scale = jnp.zeros((n, tok), f32)
    for k in range(top):
        hit = index[k : k + 1, :] == expert_row
        chosen = jnp.where(hit, 1.0, chosen)
        scale = jnp.where(hit, weights[k : k + 1, :], scale)
    earlier = (
        lax.broadcasted_iota(jnp.int32, (tok, tok), 0)
        < lax.broadcasted_iota(jnp.int32, (tok, tok), 1)
    ).astype(bf16)
    slot = jnp.dot(chosen.astype(bf16), earlier, preferred_element_type=f32)
    slot = jnp.where(chosen > 0.5, slot, -1.0)
    scale = scale.astype(bf16).astype(f32)
    pad = jnp.zeros((6, tok), f32)
    for e in range(n):
        table_send[e] = jnp.concatenate([slot[e : e + 1], scale[e : e + 1], pad], axis=0)
    table_recv[me] = table_send[me]

    def table_copy(to, source):
        return pltpu.make_async_remote_copy(
            src_ref=table_send.at[to],
            dst_ref=table_recv.at[source],
            send_sem=table_send_sem.at[to],
            recv_sem=table_recv_sem.at[source],
            device_id={"expert": to},
            device_id_type=MESH,
        )

    def others(act_on):
        def body(i, _):
            act_on((me + i) % n)
            return 0

        lax.fori_loop(1, n, body, 0)

    others(lambda to: table_copy(to, me).start())

    local[0].wait()
    low[...] = lax.dot_general(
        hidden[...], first_ref[...], (((1,), (1,)), ((), ())), preferred_element_type=f32
    ).astype(bf16)
    local[1].wait()
    first_sum[...] = jnp.zeros_like(first_sum)
    router_sum[...] = jnp.zeros_like(router_sum)
    second_out[...] = jnp.zeros_like(second_out)

    tile = 512
    tiles = feat // tile

    def output_tile(i):
        at = pl.ds(pl.multiple_of(i * tile, tile), tile)
        expert_out[:, at] = (
            jnp.dot(hidden[...], weight[:, at], preferred_element_type=f32)
            + adapter_scale
            * jnp.dot(low[...], second_ref[:, at], preferred_element_type=f32)
        ).astype(bf16)

    def dot_copy(to, source):
        return pltpu.make_async_remote_copy(
            src_ref=dot_send.at[to],
            dst_ref=dot_recv.at[source],
            send_sem=dot_send_sem.at[to],
            recv_sem=dot_recv_sem.at[source],
            device_id={"expert": to},
            device_id_type=MESH,
        )

    def chip(zz, xx):
        pair = zz * 2 + xx

        def arrived(part, _):
            move(SIBLING, zz, xx, 1 - c, part).wait_recv()
            return 0

        lax.fori_loop(0, PARTS, arrived, 0)
        both = tokens[pair]
        at = pl.ds(pl.multiple_of(pair * 2 * cap, 2 * cap), 2 * cap)
        nt = (((1,), (1,)), ((), ()))
        inner = lax.dot_general(expert_out[at, :], both, nt, preferred_element_type=f32)
        back = lax.dot_general(second_ref[...], both, nt, preferred_element_type=f32)
        t0, t1 = table_recv[2 * pair], table_recv[2 * pair + 1]
        slots = jnp.concatenate([t0[0:1], jnp.where(t1[0:1] < 0.0, -1.0, t1[0:1] + cap)], axis=1)
        scales = jnp.concatenate([t0[1:2], t1[1:2]], axis=1)
        number = lax.broadcasted_iota(jnp.int32, (2 * cap, 2 * tok), 0).astype(f32)
        match = number == slots
        dots = jnp.sum(jnp.where(match, inner, 0.0), axis=0, keepdims=True)
        for sub in range(2):
            to = 2 * pair + sub
            dot_send[to] = jnp.broadcast_to(dots[:, sub * tok : (sub + 1) * tok], (8, tok))

            @pl.when(to != me)
            def _():
                dot_copy(to, me).start()

            @pl.when(to == me)
            def _():
                dot_recv[to] = dot_send[to]

        one_hot = match.astype(bf16)
        back = (back * scales).astype(bf16)
        back = lax.dot_general(back, one_hot, nt, preferred_element_type=f32).astype(bf16)
        first_sum[...] += jnp.dot(back, hidden[at, :], preferred_element_type=f32)
        spread = lax.dot_general(
            low[at, :], one_hot, (((0,), (0,)), ((), ())), preferred_element_type=f32
        )
        spread = (adapter_scale * spread * scales).astype(bf16)
        second_out[...] += jnp.dot(spread, both, preferred_element_type=f32)

    def along(distance, part, act_on):
        @pl.when(z >= distance)
        def _():
            zz = z - distance
            act_on(zz, part, UP, z < NZ - 1)

        @pl.when(z + distance < NZ)
        def _():
            zz = z + distance
            act_on(zz, part, DOWN, z > 0)

    def by_line(zz, part):
        return part >= jnp.where((zz == 0) | (zz == 3), 6, 7)

    def pass_on(zz, part, kind, more, act_on=start):
        if act_on is start:
            move(kind, zz, x, c, part).wait_recv()

        @pl.when(more)
        def _():
            act_on(move(kind, zz, x, c, part))

        @pl.when(jnp.logical_not(by_line(zz, part)))
        def _():
            act_on(move(ACROSS, zz, x, c, part))

        act_on(move(SIBLING, zz, x, c, part))

    def cross(zz, part, kind, more, act_on=start):
        if act_on is start:
            move(ACROSS, zz, 1 - x, c, part).wait_recv()

        @pl.when(more & by_line(zz, part))
        def _():
            act_on(move(kind, zz, 1 - x, c, part))

        act_on(move(SIBLING, zz, 1 - x, c, part))

    def cross_own(part, act_on=start):
        if act_on is start:
            move(ACROSS, z, 1 - x, c, part).wait_recv()
        inject = by_line(z, part)

        @pl.when(inject & (z < NZ - 1))
        def _():
            act_on(move(UP, z, 1 - x, c, part))

        @pl.when(inject & (z > 0))
        def _():
            act_on(move(DOWN, z, 1 - x, c, part))

        act_on(move(SIBLING, z, 1 - x, c, part))

    def chips_of(phase, which):
        side = which % 2
        distance = jnp.where(which < 2, phase, phase + 1)
        zz = jnp.where(side == 0, z - distance, z + distance)
        xx = jnp.where(which < 2, 1 - x, x)
        mine = (phase == 0) & (which == 1)
        xx = jnp.where(mine, x, xx)
        return zz, xx, (zz >= 0) & (zz < NZ)

    def first_phase(part, _):
        along(1, part, pass_on)
        for j in range(2):
            i = part * 2 + j

            @pl.when(i < tiles)
            def _():
                output_tile(i)

        cross_own(part)
        return 0

    lax.fori_loop(0, PARTS, first_phase, 0)
    local[2].wait()
    others(lambda source: table_copy(source, source).wait_recv())

    def later(step, _):
        phase, part = step // PARTS, step % PARTS

        along(phase + 1, part, pass_on)
        zz, xx, there = chips_of(phase - 1, part)

        @pl.when(there & (part < 4))
        def _():
            chip(zz, xx)

        along(phase, part, cross)
        return 0

    lax.fori_loop(PARTS, NZ * PARTS, later, 0)
    for side in range(2):
        zz, xx, there = chips_of(NZ - 1, side)

        @pl.when(there)
        def _():
            chip(zz, xx)

    first_out[...] = adapter_scale * first_sum[...]
    local[3].wait()
    others(lambda source: dot_copy(source, source).wait_recv())
    dots = dot_recv[:, 0, :]
    grads = []
    for k in range(top):
        hit = index[k : k + 1, :] == expert_row
        grads.append(jnp.sum(jnp.where(hit, dots, 0.0), axis=0, keepdims=True))
    weight_grad = jnp.concatenate(grads, axis=0)
    mixed = jnp.sum(weights * weight_grad, axis=0, keepdims=True)
    csg = (weight_grad - mixed) / score_sum
    csg_ref[...] = csg
    logit = (csg * scores * (1.0 - scores)).astype(bf16).astype(f32)
    router = jnp.zeros((n, tok), f32)
    for k in range(top):
        router = jnp.where(index[k : k + 1, :] == expert_row, logit[k : k + 1, :], router)
    partial = jnp.dot(router.astype(bf16), act[...], preferred_element_type=f32)
    for j in range(feat // 128):
        router_sum[:, j, :] = partial[:, j * 128 : (j + 1) * 128]
    router_send[...] = router_sum[...].astype(bf16)
    router_recv[me] = router_send[me]

    def router_copy(to, source):
        return pltpu.make_async_remote_copy(
            src_ref=router_send.at[to],
            dst_ref=router_recv.at[source],
            send_sem=router_send_sem.at[to],
            recv_sem=router_recv_sem.at[source],
            device_id={"expert": to},
            device_id_type=MESH,
        )

    others(lambda to: router_copy(to, me).start())

    def drain(part, _):
        own(part, sent)
        cross_own(part, sent)
        return 0

    lax.fori_loop(0, PARTS, drain, 0)

    def drain_later(step, _):
        distance, part = step // PARTS, step % PARTS
        along(distance, part, functools.partial(pass_on, act_on=sent))
        along(distance, part, functools.partial(cross, act_on=sent))
        return 0

    lax.fori_loop(PARTS, NZ * PARTS, drain_later, 0)
    others(lambda to: table_copy(to, me).wait_send())
    others(lambda to: dot_copy(to, me).wait_send())
    others(lambda source: router_copy(source, source).wait_recv())
    total = jnp.sum(router_recv[...].astype(f32), axis=0)
    router_out[...] = total[: feat // 128]
    others(lambda to: router_copy(to, me).wait_send())


def hand_over(csg_ref, first_ref, second_ref, router_ref, csg_out, first_out, second_out, router_out):
    csg_out[...] = csg_ref[...]
    first_out[...] = first_ref[...]
    second_out[...] = second_ref[...]
    for j in range(router_ref.shape[0]):
        router_out[:, j * 128 : (j + 1) * 128] = router_ref[j : j + 1, :]


def per_device_gather(
    output_gradient, activations, scores, chosen_expert_index,
    frozen_down_weight, adapter_first, adapter_second, stored_hidden_rows,
):
    n = NZ * NX * NC
    tok, feat = output_gradient.shape
    units, rank = adapter_first.shape[1:]
    slots = stored_hidden_rows.shape[1]
    vmem = pl.BlockSpec(memory_space=pltpu.VMEM)
    hbm = pl.BlockSpec(memory_space=pl.ANY)
    f32, bf16 = jnp.float32, jnp.bfloat16
    padded = -(-feat // 2048) * 16
    dma = pltpu.SemaphoreType.DMA
    csg, first, second, router = pl.pallas_call(
        gather_kernel,
        out_shape=(
            jax.ShapeDtypeStruct(scores.shape[::-1], f32),
            jax.ShapeDtypeStruct((rank, units), f32),
            jax.ShapeDtypeStruct((rank, feat), f32),
            jax.ShapeDtypeStruct((feat // 128, 128), f32),
        ),
        in_specs=[hbm, hbm, vmem, vmem, hbm, vmem, vmem, hbm],
        out_specs=(vmem,) * 4,
        scratch_shapes=[
            pltpu.VMEM((NZ * NX, NC * tok, feat), bf16),
            pltpu.VMEM((units, feat), bf16),
            pltpu.VMEM((slots, units), bf16),
            pltpu.VMEM((tok, feat), bf16),
            pltpu.VMEM((slots, feat), bf16),
            pltpu.VMEM((slots, rank), bf16),
            pltpu.VMEM((rank, units), f32),
            pltpu.VMEM((n, 8, tok), f32),
            pltpu.VMEM((n, 8, tok), f32),
            pltpu.VMEM((n, 8, tok), f32),
            pltpu.VMEM((n, 8, tok), f32),
            pltpu.VMEM((n, padded, 128), f32),
            pltpu.VMEM((n, padded, 128), bf16),
            pltpu.VMEM((n, padded, 128), bf16),
            dma((4, n, PARTS)),
            dma((n, PARTS)),
            dma((n,)),
            dma((n,)),
            dma((n,)),
            dma((n,)),
            dma((n,)),
            dma((n,)),
            dma((4,)),
        ],
        compiler_params=pltpu.CompilerParams(
            collective_id=0, has_side_effects=True, vmem_limit_bytes=60 * 1024 * 1024
        ),
        cost_estimate=pl.CostEstimate(
            flops=2 * slots * units * feat, bytes_accessed=2 * units * feat, transcendentals=0
        ),
    )(
        output_gradient, activations, scores.T, chosen_expert_index.T,
        frozen_down_weight[0], adapter_first[0].T, adapter_second[0], stored_hidden_rows[0],
    )
    csg, first, second, router = pl.pallas_call(
        hand_over,
        out_shape=(
            jax.ShapeDtypeStruct(csg.shape, f32),
            jax.ShapeDtypeStruct(first.shape, f32),
            jax.ShapeDtypeStruct(second.shape, f32),
            jax.ShapeDtypeStruct((1, feat), f32),
        ),
        in_specs=[vmem] * 4,
        out_specs=(vmem,) * 4,
    )(csg, first, second, router)
    return csg.T, first.T[None], second[None], router


def recompute_every_expert(hidden_activation, lowrank_hidden, expert_down_matrix, second_factor):
    return jnp.dot(
        hidden_activation, expert_down_matrix, preferred_element_type=jnp.float32
    ) + adapter_scale * jnp.dot(lowrank_hidden, second_factor, preferred_element_type=jnp.float32)


def per_device(
    output_gradient,
    activations,
    scores,
    chosen_expert_index,
    frozen_down_weight,
    adapter_first,
    adapter_second,
    stored_hidden_rows,
):
    devices = lax.axis_size("expert")
    exp_dev = frozen_down_weight.shape[0]
    slot_rows = stored_hidden_rows.shape[1]
    capacity = slot_rows // devices
    experts = exp_dev * devices
    tokens_dev = output_gradient.shape[0]
    chosen = scores.shape[1]
    features = output_gradient.shape[1]
    score_sum = jnp.sum(scores, axis=1, keepdims=True)
    weights = scores / score_sum
    slot_weight = weights.astype(jnp.bfloat16)
    flat_ids = chosen_expert_index.reshape(-1)
    one_hot = (flat_ids[:, None] == jnp.arange(experts, dtype=jnp.int32)[None, :]).astype(jnp.int32)
    slot_index = jnp.sum((jnp.cumsum(one_hot, axis=0) - 1) * one_hot, axis=1)
    position = flat_ids * capacity + slot_index
    repeated = jnp.repeat(output_gradient, chosen, axis=0)
    send_rows = jnp.zeros((experts * capacity, features), jnp.bfloat16).at[position].set(repeated)
    send_scale = (
        jnp.zeros((experts * capacity,), jnp.bfloat16).at[position].set(slot_weight.reshape(-1))
    )
    send_rows = send_rows.reshape(devices, exp_dev, capacity, features)
    send_scale = send_scale.reshape(devices, exp_dev, capacity)
    expert_number = 0
    hidden_activation = stored_hidden_rows[expert_number]
    lowrank_hidden = jnp.dot(
        hidden_activation, adapter_first[expert_number], preferred_element_type=jnp.float32
    ).astype(jnp.bfloat16)
    expert_output = recompute_every_expert(
        hidden_activation,
        lowrank_hidden,
        frozen_down_weight[expert_number],
        adapter_second[expert_number],
    )
    lows = [lowrank_hidden]
    outputs = [expert_output]
    recv_rows, recv_scale = (
        lax.all_to_all(send_rows, "expert", split_axis=0, concat_axis=0, tiled=True),
        lax.all_to_all(send_scale, "expert", split_axis=0, concat_axis=0, tiled=True),
    )
    expert_number = 0
    slot_grad = recv_rows[:, expert_number].reshape(slot_rows, features)
    slot_scale = recv_scale[:, expert_number].reshape(slot_rows)
    slot_inner_product = jnp.sum(slot_grad.astype(jnp.float32) * outputs[expert_number], axis=1)
    scaled_output_gradient = (
        slot_scale.astype(jnp.float32)[:, None] * slot_grad.astype(jnp.float32)
    ).astype(jnp.bfloat16)
    backward_lowrank = lax.dot_general(
        scaled_output_gradient,
        adapter_second[expert_number],
        (((1,), (1,)), ((), ())),
        preferred_element_type=jnp.float32,
    ).astype(jnp.bfloat16)
    first_factor_gradient = adapter_scale * lax.dot_general(
        stored_hidden_rows[expert_number],
        backward_lowrank,
        (((0,), (0,)), ((), ())),
        preferred_element_type=jnp.float32,
    )
    second_factor_gradient = adapter_scale * lax.dot_general(
        lows[expert_number],
        scaled_output_gradient,
        (((0,), (0,)), ((), ())),
        preferred_element_type=jnp.float32,
    )
    dots = [slot_inner_product.reshape(devices, capacity)]
    grads_a = [first_factor_gradient]
    grads_b = [second_factor_gradient]
    dot_table = jnp.stack(dots, axis=1)
    returned = lax.all_to_all(dot_table, "expert", split_axis=0, concat_axis=0, tiled=True)
    weight_grad = returned.reshape(experts * capacity)[position].reshape(tokens_dev, chosen)
    mixed = jnp.sum(weights * weight_grad, axis=1, keepdims=True)
    chosen_score_gradient = (weight_grad - mixed) / score_sum
    logit_grad = (chosen_score_gradient * scores * (1.0 - scores)).astype(jnp.bfloat16)
    matches = chosen_expert_index[None, :, :] == jnp.arange(experts, dtype=jnp.int32)[:, None, None]
    router_matrix = jnp.sum(
        jnp.where(matches, logit_grad.astype(jnp.float32)[None, :, :], 0.0), axis=2
    ).astype(jnp.bfloat16)
    router_weight_gradient = lax.psum_scatter(
        jnp.dot(router_matrix, activations, preferred_element_type=jnp.float32),
        "expert",
        scatter_dimension=0,
        tiled=True,
    )
    return (
        chosen_score_gradient,
        jnp.stack(grads_a, axis=0),
        jnp.stack(grads_b, axis=0),
        router_weight_gradient,
    )


def solution(mesh):
    placed = (
        P(("groups", "expert"), None),
        P(("groups", "expert"), None),
        P(("groups", "expert"), None),
        P(("groups", "expert"), None),
        P("expert", None, None),
        P("expert", None, None),
        P("expert", None, None),
        P(("groups", "expert"), None, None),
    )
    small = mesh.shape["expert"] == NZ * NX * NC
    return jax.shard_map(
        per_device_gather if small else per_device,
        mesh=mesh,
        in_specs=placed,
        out_specs=(
            P(("groups", "expert"), None),
            P(("groups", "expert"), None, None),
            P(("groups", "expert"), None, None),
            P(("groups", "expert"), None),
        ),
        check_vma=False,
    )
```

```python
import functools

import jax
import jax.numpy as jnp
from jax import lax
from jax.experimental import pallas as pl
from jax.experimental.pallas import tpu as pltpu
from jax.sharding import PartitionSpec as P

MESH = pl.DeviceIdType.MESH
adapter_scale = 2.0

NZ, NX, NC = 4, 2, 2
PARTS = 8
UP, DOWN, ACROSS, SIBLING = range(4)


def gather_kernel(
    grad_hbm, act_hbm, scores_ref, index_ref, weight_hbm, first_ref, second_ref, hidden_hbm,
    csg_ref, first_out, second_out, router_out,
    tokens, weight, hidden, act, expert_out, low, first_sum,
    table_send, table_recv, dot_send, dot_recv, router_sum, router_send, router_recv,
    block_send_sem, block_recv_sem, table_send_sem, table_recv_sem,
    dot_send_sem, dot_recv_sem, router_send_sem, router_recv_sem, local_sem,
):
    n = NZ * NX * NC
    tok, feat = grad_hbm.shape
    top = scores_ref.shape[0]
    rank = second_ref.shape[0]
    units = weight.shape[0]
    cap = hidden.shape[0] // n
    rows = tok // PARTS
    me = lax.axis_index("expert")
    z, x, c = me // 4, (me // 2) % 2, me % 2
    f32, bf16 = jnp.float32, jnp.bfloat16

    barrier = pltpu.get_barrier_semaphore()

    def greet(i, _):
        pl.semaphore_signal(
            barrier, inc=1, device_id={"expert": (me + i) % n}, device_id_type=MESH
        )
        return 0

    local = [
        pltpu.make_async_copy(hidden_hbm, hidden, local_sem.at[0]),
        pltpu.make_async_copy(weight_hbm, weight, local_sem.at[1]),
        pltpu.make_async_copy(
            grad_hbm,
            tokens.at[z * 2 + x, pl.ds(pl.multiple_of(c * tok, tok), tok)],
            local_sem.at[2],
        ),
        pltpu.make_async_copy(act_hbm, act, local_sem.at[3]),
    ]
    for copy in local:
        copy.start()
    lax.fori_loop(1, n, greet, 0)
    pl.semaphore_wait(barrier, n - 1)

    def piece(zz, xx, cc, part):
        return tokens.at[
            zz * 2 + xx, pl.ds(pl.multiple_of(cc * tok + part * rows, rows), rows)
        ]

    def move(kind, zz, xx, cc, part, source=None):
        target = {
            UP: me + 4, DOWN: me - 4, ACROSS: z * 4 + (1 - x) * 2 + c, SIBLING: z * 4 + x * 2 + 1 - c,
        }[kind]
        block = zz * 4 + xx * 2 + cc
        place = piece(zz, xx, cc, part)
        return pltpu.make_async_remote_copy(
            src_ref=place if source is None else source,
            dst_ref=place,
            send_sem=block_send_sem.at[kind, block, part],
            recv_sem=block_recv_sem.at[block, part],
            device_id={"expert": target},
            device_id_type=MESH,
        )

    def own(part, act_on):
        source = grad_hbm.at[pl.ds(pl.multiple_of(part * rows, rows), rows)]
        act_on(move(ACROSS, z, x, c, part, source))

        @pl.when(z < NZ - 1)
        def _():
            act_on(move(UP, z, x, c, part, source))

        @pl.when(z > 0)
        def _():
            act_on(move(DOWN, z, x, c, part, source))

        act_on(move(SIBLING, z, x, c, part, source))

    def start(copy):
        copy.start()

    def sent(copy):
        copy.wait_send()

    def own_start(part, _):
        own(part, start)
        return 0

    lax.fori_loop(0, PARTS, own_start, 0)

    scores = scores_ref[...]
    index = index_ref[...]
    score_sum = jnp.sum(scores, axis=0, keepdims=True)
    weights = scores / score_sum
    expert_row = lax.broadcasted_iota(jnp.int32, (n, tok), 0)
    chosen = jnp.zeros((n, tok), f32)
    scale = jnp.zeros((n, tok), f32)
    for k in range(top):
        hit = index[k : k + 1, :] == expert_row
        chosen = jnp.where(hit, 1.0, chosen)
        scale = jnp.where(hit, weights[k : k + 1, :], scale)
    earlier = (
        lax.broadcasted_iota(jnp.int32, (tok, tok), 0)
        < lax.broadcasted_iota(jnp.int32, (tok, tok), 1)
    ).astype(bf16)
    slot = jnp.dot(chosen.astype(bf16), earlier, preferred_element_type=f32)
    slot = jnp.where(chosen > 0.5, slot, -1.0)
    scale = scale.astype(bf16).astype(f32)
    pad = jnp.zeros((6, tok), f32)
    for e in range(n):
        table_send[e] = jnp.concatenate([slot[e : e + 1], scale[e : e + 1], pad], axis=0)
    table_recv[me] = table_send[me]

    def table_copy(to, source):
        return pltpu.make_async_remote_copy(
            src_ref=table_send.at[to],
            dst_ref=table_recv.at[source],
            send_sem=table_send_sem.at[to],
            recv_sem=table_recv_sem.at[source],
            device_id={"expert": to},
            device_id_type=MESH,
        )

    def others(act_on):
        def body(i, _):
            act_on((me + i) % n)
            return 0

        lax.fori_loop(1, n, body, 0)

    others(lambda to: table_copy(to, me).start())

    local[0].wait()
    low[...] = lax.dot_general(
        hidden[...], first_ref[...], (((1,), (1,)), ((), ())), preferred_element_type=f32
    ).astype(bf16)
    local[1].wait()
    first_sum[...] = jnp.zeros_like(first_sum)
    router_sum[...] = jnp.zeros_like(router_sum)
    second_out[...] = jnp.zeros_like(second_out)

    tile = 512
    tiles = feat // tile

    def output_tile(i):
        at = pl.ds(pl.multiple_of(i * tile, tile), tile)
        expert_out[:, at] = (
            jnp.dot(hidden[...], weight[:, at], preferred_element_type=f32)
            + adapter_scale
            * jnp.dot(low[...], second_ref[:, at], preferred_element_type=f32)
        ).astype(bf16)

    def dot_copy(to, source):
        return pltpu.make_async_remote_copy(
            src_ref=dot_send.at[to],
            dst_ref=dot_recv.at[source],
            send_sem=dot_send_sem.at[to],
            recv_sem=dot_recv_sem.at[source],
            device_id={"expert": to},
            device_id_type=MESH,
        )

    def chip(zz, xx):
        pair = zz * 2 + xx

        def arrived(part, _):
            move(SIBLING, zz, xx, 1 - c, part).wait_recv()
            return 0

        lax.fori_loop(0, PARTS, arrived, 0)
        both = tokens[pair]
        at = pl.ds(pl.multiple_of(pair * 2 * cap, 2 * cap), 2 * cap)
        nt = (((1,), (1,)), ((), ()))
        inner = lax.dot_general(expert_out[at, :], both, nt, preferred_element_type=f32)
        back = lax.dot_general(second_ref[...], both, nt, preferred_element_type=f32)
        t0, t1 = table_recv[2 * pair], table_recv[2 * pair + 1]
        slots = jnp.concatenate([t0[0:1], jnp.where(t1[0:1] < 0.0, -1.0, t1[0:1] + cap)], axis=1)
        scales = jnp.concatenate([t0[1:2], t1[1:2]], axis=1)
        number = lax.broadcasted_iota(jnp.int32, (2 * cap, 2 * tok), 0).astype(f32)
        match = number == slots
        dots = jnp.sum(jnp.where(match, inner, 0.0), axis=0, keepdims=True)
        for sub in range(2):
            to = 2 * pair + sub
            dot_send[to] = jnp.broadcast_to(dots[:, sub * tok : (sub + 1) * tok], (8, tok))

            @pl.when(to != me)
            def _():
                dot_copy(to, me).start()

            @pl.when(to == me)
            def _():
                dot_recv[to] = dot_send[to]

        one_hot = match.astype(bf16)
        back = (back * scales).astype(bf16)
        back = lax.dot_general(back, one_hot, nt, preferred_element_type=f32).astype(bf16)
        first_sum[...] += jnp.dot(back, hidden[at, :], preferred_element_type=f32)
        spread = lax.dot_general(
            low[at, :], one_hot, (((0,), (0,)), ((), ())), preferred_element_type=f32
        )
        spread = (adapter_scale * spread * scales).astype(bf16)
        second_out[...] += jnp.dot(spread, both, preferred_element_type=f32)

    def along(distance, part, act_on):
        @pl.when(z >= distance)
        def _():
            zz = z - distance
            act_on(zz, part, UP, z < NZ - 1)

        @pl.when(z + distance < NZ)
        def _():
            zz = z + distance
            act_on(zz, part, DOWN, z > 0)

    def by_line(zz, part):
        return part < jnp.where((zz == 0) | (zz == 3), 2, 1)

    def pass_on(zz, part, kind, more, act_on=start):
        if act_on is start:
            move(kind, zz, x, c, part).wait_recv()

        @pl.when(more)
        def _():
            act_on(move(kind, zz, x, c, part))

        @pl.when(jnp.logical_not(by_line(zz, part)))
        def _():
            act_on(move(ACROSS, zz, x, c, part))

        act_on(move(SIBLING, zz, x, c, part))

    def cross(zz, part, kind, more, act_on=start):
        if act_on is start:
            move(ACROSS, zz, 1 - x, c, part).wait_recv()

        @pl.when(more & by_line(zz, part))
        def _():
            act_on(move(kind, zz, 1 - x, c, part))

        act_on(move(SIBLING, zz, 1 - x, c, part))

    def cross_own(part, act_on=start):
        if act_on is start:
            move(ACROSS, z, 1 - x, c, part).wait_recv()
        inject = by_line(z, part)

        @pl.when(inject & (z < NZ - 1))
        def _():
            act_on(move(UP, z, 1 - x, c, part))

        @pl.when(inject & (z > 0))
        def _():
            act_on(move(DOWN, z, 1 - x, c, part))

        act_on(move(SIBLING, z, 1 - x, c, part))

    def chips_of(phase, which):
        side = which % 2
        distance = jnp.where(which < 2, phase, phase + 1)
        zz = jnp.where(side == 0, z - distance, z + distance)
        xx = jnp.where(which < 2, 1 - x, x)
        mine = (phase == 0) & (which == 1)
        xx = jnp.where(mine, x, xx)
        return zz, xx, (zz >= 0) & (zz < NZ)

    def first_phase(part, _):
        along(1, part, pass_on)
        for j in range(2):
            i = part * 2 + j

            @pl.when(i < tiles)
            def _():
                output_tile(i)

        cross_own(part)
        return 0

    lax.fori_loop(0, PARTS, first_phase, 0)
    local[2].wait()
    others(lambda source: table_copy(source, source).wait_recv())

    def later(step, _):
        phase, part = step // PARTS, step % PARTS

        along(phase + 1, part, pass_on)
        zz, xx, there = chips_of(phase - 1, part)

        @pl.when(there & (part < 4))
        def _():
            chip(zz, xx)

        along(phase, part, cross)
        return 0

    lax.fori_loop(PARTS, NZ * PARTS, later, 0)
    for side in range(2):
        zz, xx, there = chips_of(NZ - 1, side)

        @pl.when(there)
        def _():
            chip(zz, xx)

    first_out[...] = adapter_scale * first_sum[...]
    local[3].wait()
    others(lambda source: dot_copy(source, source).wait_recv())
    dots = dot_recv[:, 0, :]
    grads = []
    for k in range(top):
        hit = index[k : k + 1, :] == expert_row
        grads.append(jnp.sum(jnp.where(hit, dots, 0.0), axis=0, keepdims=True))
    weight_grad = jnp.concatenate(grads, axis=0)
    mixed = jnp.sum(weights * weight_grad, axis=0, keepdims=True)
    csg = (weight_grad - mixed) / score_sum
    csg_ref[...] = csg
    logit = (csg * scores * (1.0 - scores)).astype(bf16).astype(f32)
    router = jnp.zeros((n, tok), f32)
    for k in range(top):
        router = jnp.where(index[k : k + 1, :] == expert_row, logit[k : k + 1, :], router)
    partial = jnp.dot(router.astype(bf16), act[...], preferred_element_type=f32)
    for j in range(feat // 128):
        router_sum[:, j, :] = partial[:, j * 128 : (j + 1) * 128]
    router_send[...] = router_sum[...].astype(bf16)
    router_recv[me] = router_send[me]

    def router_copy(to, source):
        return pltpu.make_async_remote_copy(
            src_ref=router_send.at[to],
            dst_ref=router_recv.at[source],
            send_sem=router_send_sem.at[to],
            recv_sem=router_recv_sem.at[source],
            device_id={"expert": to},
            device_id_type=MESH,
        )

    others(lambda to: router_copy(to, me).start())

    def drain(part, _):
        own(part, sent)
        cross_own(part, sent)
        return 0

    lax.fori_loop(0, PARTS, drain, 0)

    def drain_later(step, _):
        distance, part = step // PARTS, step % PARTS
        along(distance, part, functools.partial(pass_on, act_on=sent))
        along(distance, part, functools.partial(cross, act_on=sent))
        return 0

    lax.fori_loop(PARTS, NZ * PARTS, drain_later, 0)
    others(lambda to: table_copy(to, me).wait_send())
    others(lambda to: dot_copy(to, me).wait_send())
    others(lambda source: router_copy(source, source).wait_recv())
    total = jnp.sum(router_recv[...].astype(f32), axis=0)
    router_out[...] = total[: feat // 128]
    others(lambda to: router_copy(to, me).wait_send())


def hand_over(csg_ref, first_ref, second_ref, router_ref, csg_out, first_out, second_out, router_out):
    csg_out[...] = csg_ref[...]
    first_out[...] = first_ref[...]
    second_out[...] = second_ref[...]
    for j in range(router_ref.shape[0]):
        router_out[:, j * 128 : (j + 1) * 128] = router_ref[j : j + 1, :]


def per_device_gather(
    output_gradient, activations, scores, chosen_expert_index,
    frozen_down_weight, adapter_first, adapter_second, stored_hidden_rows,
):
    n = NZ * NX * NC
    tok, feat = output_gradient.shape
    units, rank = adapter_first.shape[1:]
    slots = stored_hidden_rows.shape[1]
    vmem = pl.BlockSpec(memory_space=pltpu.VMEM)
    hbm = pl.BlockSpec(memory_space=pl.ANY)
    f32, bf16 = jnp.float32, jnp.bfloat16
    padded = -(-feat // 2048) * 16
    dma = pltpu.SemaphoreType.DMA
    csg, first, second, router = pl.pallas_call(
        gather_kernel,
        out_shape=(
            jax.ShapeDtypeStruct(scores.shape[::-1], f32),
            jax.ShapeDtypeStruct((rank, units), f32),
            jax.ShapeDtypeStruct((rank, feat), f32),
            jax.ShapeDtypeStruct((feat // 128, 128), f32),
        ),
        in_specs=[hbm, hbm, vmem, vmem, hbm, vmem, vmem, hbm],
        out_specs=(vmem,) * 4,
        scratch_shapes=[
            pltpu.VMEM((NZ * NX, NC * tok, feat), bf16),
            pltpu.VMEM((units, feat), bf16),
            pltpu.VMEM((slots, units), bf16),
            pltpu.VMEM((tok, feat), bf16),
            pltpu.VMEM((slots, feat), bf16),
            pltpu.VMEM((slots, rank), bf16),
            pltpu.VMEM((rank, units), f32),
            pltpu.VMEM((n, 8, tok), f32),
            pltpu.VMEM((n, 8, tok), f32),
            pltpu.VMEM((n, 8, tok), f32),
            pltpu.VMEM((n, 8, tok), f32),
            pltpu.VMEM((n, padded, 128), f32),
            pltpu.VMEM((n, padded, 128), bf16),
            pltpu.VMEM((n, padded, 128), bf16),
            dma((4, n, PARTS)),
            dma((n, PARTS)),
            dma((n,)),
            dma((n,)),
            dma((n,)),
            dma((n,)),
            dma((n,)),
            dma((n,)),
            dma((4,)),
        ],
        compiler_params=pltpu.CompilerParams(
            collective_id=0, has_side_effects=True, vmem_limit_bytes=60 * 1024 * 1024
        ),
        cost_estimate=pl.CostEstimate(
            flops=2 * slots * units * feat, bytes_accessed=2 * units * feat, transcendentals=0
        ),
    )(
        output_gradient, activations, scores.T, chosen_expert_index.T,
        frozen_down_weight[0], adapter_first[0].T, adapter_second[0], stored_hidden_rows[0],
    )
    csg, first, second, router = pl.pallas_call(
        hand_over,
        out_shape=(
            jax.ShapeDtypeStruct(csg.shape, f32),
            jax.ShapeDtypeStruct(first.shape, f32),
            jax.ShapeDtypeStruct(second.shape, f32),
            jax.ShapeDtypeStruct((1, feat), f32),
        ),
        in_specs=[vmem] * 4,
        out_specs=(vmem,) * 4,
    )(csg, first, second, router)
    return csg.T, first.T[None], second[None], router


def recompute_every_expert(hidden_activation, lowrank_hidden, expert_down_matrix, second_factor):
    return jnp.dot(
        hidden_activation, expert_down_matrix, preferred_element_type=jnp.float32
    ) + adapter_scale * jnp.dot(lowrank_hidden, second_factor, preferred_element_type=jnp.float32)


def per_device(
    output_gradient,
    activations,
    scores,
    chosen_expert_index,
    frozen_down_weight,
    adapter_first,
    adapter_second,
    stored_hidden_rows,
):
    devices = lax.axis_size("expert")
    exp_dev = frozen_down_weight.shape[0]
    slot_rows = stored_hidden_rows.shape[1]
    capacity = slot_rows // devices
    experts = exp_dev * devices
    tokens_dev = output_gradient.shape[0]
    chosen = scores.shape[1]
    features = output_gradient.shape[1]
    score_sum = jnp.sum(scores, axis=1, keepdims=True)
    weights = scores / score_sum
    slot_weight = weights.astype(jnp.bfloat16)
    flat_ids = chosen_expert_index.reshape(-1)
    one_hot = (flat_ids[:, None] == jnp.arange(experts, dtype=jnp.int32)[None, :]).astype(jnp.int32)
    slot_index = jnp.sum((jnp.cumsum(one_hot, axis=0) - 1) * one_hot, axis=1)
    position = flat_ids * capacity + slot_index
    repeated = jnp.repeat(output_gradient, chosen, axis=0)
    send_rows = jnp.zeros((experts * capacity, features), jnp.bfloat16).at[position].set(repeated)
    send_scale = (
        jnp.zeros((experts * capacity,), jnp.bfloat16).at[position].set(slot_weight.reshape(-1))
    )
    send_rows = send_rows.reshape(devices, exp_dev, capacity, features)
    send_scale = send_scale.reshape(devices, exp_dev, capacity)
    expert_number = 0
    hidden_activation = stored_hidden_rows[expert_number]
    lowrank_hidden = jnp.dot(
        hidden_activation, adapter_first[expert_number], preferred_element_type=jnp.float32
    ).astype(jnp.bfloat16)
    expert_output = recompute_every_expert(
        hidden_activation,
        lowrank_hidden,
        frozen_down_weight[expert_number],
        adapter_second[expert_number],
    )
    lows = [lowrank_hidden]
    outputs = [expert_output]
    recv_rows, recv_scale = (
        lax.all_to_all(send_rows, "expert", split_axis=0, concat_axis=0, tiled=True),
        lax.all_to_all(send_scale, "expert", split_axis=0, concat_axis=0, tiled=True),
    )
    expert_number = 0
    slot_grad = recv_rows[:, expert_number].reshape(slot_rows, features)
    slot_scale = recv_scale[:, expert_number].reshape(slot_rows)
    slot_inner_product = jnp.sum(slot_grad.astype(jnp.float32) * outputs[expert_number], axis=1)
    scaled_output_gradient = (
        slot_scale.astype(jnp.float32)[:, None] * slot_grad.astype(jnp.float32)
    ).astype(jnp.bfloat16)
    backward_lowrank = lax.dot_general(
        scaled_output_gradient,
        adapter_second[expert_number],
        (((1,), (1,)), ((), ())),
        preferred_element_type=jnp.float32,
    ).astype(jnp.bfloat16)
    first_factor_gradient = adapter_scale * lax.dot_general(
        stored_hidden_rows[expert_number],
        backward_lowrank,
        (((0,), (0,)), ((), ())),
        preferred_element_type=jnp.float32,
    )
    second_factor_gradient = adapter_scale * lax.dot_general(
        lows[expert_number],
        scaled_output_gradient,
        (((0,), (0,)), ((), ())),
        preferred_element_type=jnp.float32,
    )
    dots = [slot_inner_product.reshape(devices, capacity)]
    grads_a = [first_factor_gradient]
    grads_b = [second_factor_gradient]
    dot_table = jnp.stack(dots, axis=1)
    returned = lax.all_to_all(dot_table, "expert", split_axis=0, concat_axis=0, tiled=True)
    weight_grad = returned.reshape(experts * capacity)[position].reshape(tokens_dev, chosen)
    mixed = jnp.sum(weights * weight_grad, axis=1, keepdims=True)
    chosen_score_gradient = (weight_grad - mixed) / score_sum
    logit_grad = (chosen_score_gradient * scores * (1.0 - scores)).astype(jnp.bfloat16)
    matches = chosen_expert_index[None, :, :] == jnp.arange(experts, dtype=jnp.int32)[:, None, None]
    router_matrix = jnp.sum(
        jnp.where(matches, logit_grad.astype(jnp.float32)[None, :, :], 0.0), axis=2
    ).astype(jnp.bfloat16)
    router_weight_gradient = lax.psum_scatter(
        jnp.dot(router_matrix, activations, preferred_element_type=jnp.float32),
        "expert",
        scatter_dimension=0,
        tiled=True,
    )
    return (
        chosen_score_gradient,
        jnp.stack(grads_a, axis=0),
        jnp.stack(grads_b, axis=0),
        router_weight_gradient,
    )


def solution(mesh):
    placed = (
        P(("groups", "expert"), None),
        P(("groups", "expert"), None),
        P(("groups", "expert"), None),
        P(("groups", "expert"), None),
        P("expert", None, None),
        P("expert", None, None),
        P("expert", None, None),
        P(("groups", "expert"), None, None),
    )
    small = mesh.shape["expert"] == NZ * NX * NC
    return jax.shard_map(
        per_device_gather if small else per_device,
        mesh=mesh,
        in_specs=placed,
        out_specs=(
            P(("groups", "expert"), None),
            P(("groups", "expert"), None, None),
            P(("groups", "expert"), None, None),
            P(("groups", "expert"), None),
        ),
        check_vma=False,
    )
```
